32 devices in a mesh: seq: 16 (over z, x, core), head: 2 (over y).
Axes of the slice: x: 2, y: 2, z: 4, core: 2. Of those that a mesh axis runs over, the one named last changes fastest.
Arguments:
- normed: bfloat16 [8192, 5376], P('seq'), may hold values from -6 to 6
- cotangent: bfloat16 [8192, 2048], P('seq', 'head'), may hold values from -6 to 6
- qkv_master: float32 [5376, 8, 512], P('seq', 'head'), may hold values from -0.078125 to 0.078125
- adam_first: float32 [5376, 8, 512], P('seq', 'head'), may hold values from -6 to 6
- adam_second: float32 [5376, 8, 512], P('seq', 'head'), may hold values from 0.5 to 20
- skip_flag: int32 [8], replicated, may hold values 0 or 1
- scale_exponent: int32 [1], replicated, may hold values from 4 to 8
Outputs:
- attn_out: bfloat16 [8192, 2048], P('seq', 'head')
- d_tokens: bfloat16 [8192, 5376], P(('seq', 'head'))
- new_master: float32 [5376, 8, 512], P('seq', 'head')
- new_first: float32 [5376, 8, 512], P('seq', 'head')
- new_second: float32 [5376, 8, 512], P('seq', 'head')
The draws below stay inside these ranges and needn't reach their ends.
All inputs are finite; a program needn't handle non-finite values.
Results may differ from the reference program's by a relative error of at most 0.0095.
Values may be sent and summed in bfloat16 or wider, within the bound.
A program may use at most 256 MiB of HBM per device.

```python
import math
import jax
import jax.numpy as jnp
from jax import lax

D = 5376
HEAD_DIM = 128
ATTEND_SPAN = 1024
ATTN_SCALAR = 168
KV_HEADS = 8
Q_PER_KV = 2
ADAM_STEP = 1000
TOK_DEV = 512
TOKENS = 8192
Q_HEADS = 16
GROUP_COLS = 512


def set_ends(entries, own_key, low, largest):
    shape = entries.shape
    spot = [jax.random.randint(jax.random.fold_in(own_key, axis), (), 0, shape[axis]) for axis in range(len(shape))]
    entries = entries.at[tuple(spot)].set(low)
    longest = shape.index(max(shape))
    spot[longest] = (spot[longest] + 1) % shape[longest]
    return entries.at[tuple(spot)].set(largest)


def strengthened(drawn, key, source, target, shards_of, factor):
    def block_of(axis_at):
        return (jnp.arange(drawn.shape[axis_at]) // (drawn.shape[axis_at] // shards_of)).reshape((-1,) + (1,) * (drawn.ndim - 1 - axis_at))

    one_side = jax.random.permutation(key, shards_of)[block_of(target)]
    far = (block_of(target) + shards_of // 2) % shards_of
    return jnp.where((block_of(source) == one_side) | (block_of(source) == far), factor * drawn, drawn)


def shard_levels(rng, shape, split, least, top_value):
    level = 1.0
    for dim, shards_of in split:
        draws = jax.random.uniform(jax.random.fold_in(jax.random.fold_in(rng, 6), dim), (shards_of,), jnp.float32, least / len(split), top_value / len(split))
        level = level * jnp.repeat(jnp.exp(draws), shape[dim] // shards_of).reshape((-1,) + (1,) * (len(shape) - 1 - dim))
    return level


def normal_values(rng, dims, deviation, most, pieces=(), kind=jnp.bfloat16):
    entries = jax.random.normal(rng, dims, jnp.float32) * deviation
    if len(pieces) > 0:
        entries = shard_levels(rng, dims, pieces, -0.22, 0.18) * entries
    return jnp.clip(entries, min=-most, max=most).astype(kind)


def gaussian_with(key, shape, scale, reach, cuts, heavy, kind=jnp.bfloat16):
    drawn = scale * jax.random.normal(key, shape, jnp.float32)
    if cuts:
        drawn = drawn * shard_levels(key, shape, cuts, -0.22, 0.18)
    return jnp.clip(strengthened(drawn, jax.random.fold_in(key, 3), *heavy), -reach, reach).astype(kind)


def setup_inputs(seed: int = 0) -> dict:
    arg_keys = jax.random.split(jax.random.key(seed), 8)
    normed = gaussian_with(arg_keys[0], (TOKENS, D), 1.0, 6.0, ((0, 16),), (0, 1, 16, 2.0))
    cotangent = normal_values(arg_keys[1], (TOKENS, Q_HEADS * HEAD_DIM), 1.0, 6.0, ((0, 16), (1, 2)))
    qkv_master = normal_values(arg_keys[2], (D, KV_HEADS, GROUP_COLS), D ** -0.5, 0.078125, ((0, 16), (1, 2)), jnp.float32)
    adam_first = normal_values(arg_keys[3], (D, KV_HEADS, GROUP_COLS), 1.0, 6.0, ((0, 16), (1, 2)), jnp.float32)
    adam_second = jnp.clip(jnp.exp(math.log(20.0) - 3.6888795 * jax.random.uniform(arg_keys[4], (D, KV_HEADS, GROUP_COLS), jnp.float32) ** shard_levels(arg_keys[4], (D, KV_HEADS, GROUP_COLS), ((0, 16), (1, 2)), -0.2, 0.2)), 0.5, 20.0)
    skip_flag = set_ends((jax.random.randint(arg_keys[5], (KV_HEADS,), 0, 2) < 1).astype(jnp.int32), jax.random.fold_in(arg_keys[5], 1), 0, 1)
    scale_exponent = jax.random.randint(arg_keys[6], (1,), 4, 9).astype(jnp.int32)
    return {"normed": normed, "cotangent": cotangent, "qkv_master": qkv_master, "adam_first": adam_first, "adam_second": adam_second, "skip_flag": skip_flag, "scale_exponent": scale_exponent}


norm_eps = 1e-06
beta_one = 0.9
beta_two = 0.95
adam_eps = 1e-08
learn_rate = 0.01
weight_decay = 0.1

def head_norm(raw_vals):
    factor = lax.rsqrt(lax.optimization_barrier(jnp.mean(raw_vals * raw_vals, axis=-1, keepdims=True)) + norm_eps)
    return (raw_vals * factor, factor)

def norm_back(raw_vals, factor, grad_in):
    inner_mean = lax.optimization_barrier(jnp.mean(raw_vals * grad_in, axis=-1, keepdims=True))
    return factor * grad_in - raw_vals * factor * factor * factor * inner_mean

def window_kernel(query_tile, key_tile, query_start, key_start):
    score_scale = float(ATTN_SCALAR) ** (-0.5)
    scores = jnp.einsum('tgqd,lgd->gqtl', query_tile.astype(jnp.float32), key_tile.astype(jnp.float32)) * score_scale
    query_pos = query_start + jnp.arange(query_tile.shape[0], dtype=jnp.int32)
    key_pos = key_start + jnp.arange(key_tile.shape[0], dtype=jnp.int32)
    gap_len = query_pos[:, None] - key_pos[None, :]
    allowed = (key_pos[None, :] >= 0) & (gap_len >= 0) & (gap_len < ATTEND_SPAN)
    return jnp.where(allowed, jnp.exp(scores), 0.0)

def reference(normed, cotangent, qkv_master, adam_first, adam_second, skip_flag, scale_exponent):
    total_rows = normed.shape[0]
    model_width = normed.shape[1]
    q_cols = Q_PER_KV * HEAD_DIM
    score_scale = float(ATTN_SCALAR) ** (-0.5)
    master16 = qkv_master.astype(jnp.bfloat16)
    flat16 = master16.reshape(model_width, KV_HEADS * GROUP_COLS)
    qkv = jnp.dot(normed, flat16, preferred_element_type=jnp.float32).reshape(total_rows, KV_HEADS, GROUP_COLS)
    q_raw = qkv[:, :, :q_cols].reshape(total_rows, KV_HEADS, Q_PER_KV, HEAD_DIM)
    k_raw = qkv[:, :, q_cols:q_cols + HEAD_DIM]
    v_raw = qkv[:, :, q_cols + HEAD_DIM:]
    q_unit, q_factor = head_norm(q_raw)
    k_unit, k_factor = head_norm(k_raw)
    queries = lax.optimization_barrier(q_unit.astype(jnp.bfloat16))
    key_tiles = lax.optimization_barrier(k_unit.astype(jnp.bfloat16))
    values = lax.optimization_barrier(v_raw.astype(jnp.bfloat16))
    scale_power = jnp.left_shift(jnp.int32(1), scale_exponent[0]).astype(jnp.float32)
    grad_out = lax.optimization_barrier((cotangent.astype(jnp.float32) * scale_power).astype(jnp.bfloat16))
    grad_out = grad_out.reshape(total_rows, KV_HEADS, Q_PER_KV, HEAD_DIM)
    pad_keys = jnp.concatenate([jnp.zeros((ATTEND_SPAN, KV_HEADS, HEAD_DIM), jnp.bfloat16), key_tiles], 0)
    pad_values = jnp.concatenate([jnp.zeros((ATTEND_SPAN, KV_HEADS, HEAD_DIM), jnp.bfloat16), values], 0)
    window_length = TOK_DEV + ATTEND_SPAN

    def single_block(carry_state, block_index):
        padded_key_gradient, padded_value_gradient = carry_state
        starting_row = (block_index * TOK_DEV).astype(jnp.int32)
        q_block = lax.dynamic_slice_in_dim(queries, starting_row, TOK_DEV, 0)
        go_block = lax.dynamic_slice_in_dim(grad_out, starting_row, TOK_DEV, 0)
        k_block = lax.dynamic_slice_in_dim(pad_keys, starting_row, window_length, 0)
        v_block = lax.dynamic_slice_in_dim(pad_values, starting_row, window_length, 0)
        kernel = window_kernel(q_block, k_block, starting_row, starting_row - ATTEND_SPAN)
        totals = lax.optimization_barrier(jnp.sum(kernel, axis=-1, keepdims=True))
        prob_tile = lax.optimization_barrier((kernel / totals).astype(jnp.bfloat16))
        attention_blend = jnp.einsum('gqtl,lgd->tgqd', prob_tile.astype(jnp.float32), v_block.astype(jnp.float32))
        row_delta = jnp.transpose(lax.optimization_barrier(jnp.sum(go_block.astype(jnp.float32) * attention_blend, axis=-1)), (1, 2, 0))
        grad_probs = jnp.einsum('tgqd,lgd->gqtl', go_block.astype(jnp.float32), v_block.astype(jnp.float32))
        grad_scores = (prob_tile.astype(jnp.float32) * (grad_probs - row_delta[..., None]) * score_scale).astype(jnp.bfloat16)
        grad_scores = lax.optimization_barrier(grad_scores).astype(jnp.float32)
        query_gradient = jnp.einsum('gqtl,lgd->tgqd', grad_scores, k_block.astype(jnp.float32))
        grad_k = jnp.einsum('gqtl,tgqd->lgd', grad_scores, q_block.astype(jnp.float32))
        value_gradient = jnp.einsum('gqtl,tgqd->lgd', prob_tile.astype(jnp.float32), go_block.astype(jnp.float32))
        old_k = lax.dynamic_slice_in_dim(padded_key_gradient, starting_row, window_length, 0)
        previous_value = lax.dynamic_slice_in_dim(padded_value_gradient, starting_row, window_length, 0)
        padded_key_gradient = lax.dynamic_update_slice_in_dim(padded_key_gradient, old_k + grad_k, starting_row, 0)
        padded_value_gradient = lax.dynamic_update_slice_in_dim(padded_value_gradient, previous_value + value_gradient, starting_row, 0)
        return ((padded_key_gradient, padded_value_gradient), (attention_blend.astype(jnp.bfloat16), query_gradient))
    zeroed_padding = jnp.zeros((ATTEND_SPAN + total_rows, KV_HEADS, HEAD_DIM), jnp.float32)
    block_numbers = jnp.arange(total_rows // TOK_DEV, dtype=jnp.int32)
    (padded_key_gradient, padded_value_gradient), (output_blocks, query_block_gradients) = lax.scan(single_block, (zeroed_padding, zeroed_padding), block_numbers)
    attn_out = output_blocks.reshape(total_rows, KV_HEADS * Q_PER_KV * HEAD_DIM)
    grad_queries = query_block_gradients.reshape(total_rows, KV_HEADS, Q_PER_KV, HEAD_DIM)
    grad_keys = padded_key_gradient[ATTEND_SPAN:]
    gradient_value_rows = padded_value_gradient[ATTEND_SPAN:]
    grad_qraw = norm_back(q_raw, q_factor, grad_queries)
    grad_kraw = norm_back(k_raw, k_factor, grad_keys)
    grad_qkv = jnp.concatenate([grad_qraw.reshape(total_rows, KV_HEADS, q_cols), grad_kraw, gradient_value_rows], -1).astype(jnp.bfloat16)
    grad_flat = grad_qkv.reshape(total_rows, KV_HEADS * GROUP_COLS)
    d_tokens = jnp.dot(grad_flat, flat16.T, preferred_element_type=jnp.float32).astype(jnp.bfloat16)
    summed = jnp.dot(normed.T, grad_flat, preferred_element_type=jnp.float32)
    gradient = (summed / scale_power).reshape(model_width, KV_HEADS, GROUP_COLS)
    first_new = beta_one * adam_first + (1.0 - beta_one) * gradient
    second_new = beta_two * adam_second + (1.0 - beta_two) * gradient * gradient
    first_fix = 1.0 - beta_one ** ADAM_STEP
    second_fix = 1.0 - beta_two ** ADAM_STEP
    update = first_new / first_fix / (jnp.sqrt(second_new / second_fix) + adam_eps)
    master_new = qkv_master - learn_rate * (update + weight_decay * qkv_master)
    applied = (skip_flag == 0)[None, :, None]
    return (attn_out, d_tokens, jnp.where(applied, master_new, qkv_master), jnp.where(applied, first_new, adam_first), jnp.where(applied, second_new, adam_second))
```

```python
import functools

import jax
import jax.numpy as jnp
from jax import lax
from jax.experimental import pallas as pl
from jax.experimental.pallas import tpu as pltpu
from jax.sharding import PartitionSpec as P

HEAD_DIM = 128
ATTEND_SPAN = 1024
ATTN_SCALAR = 168
Q_PER_KV = 2
ADAM_STEP = 1000
TILE = 128


norm_eps = 1e-06
beta_one = 0.9
beta_two = 0.95
adam_eps = 1e-08
learn_rate = 0.01
weight_decay = 0.1
score_scale = float(ATTN_SCALAR) ** (-0.5)
log2_e = 1.4426950408889634


def shifted(block, axis, distance):
    devices = range(lax.axis_size(axis))
    route = [(i - distance, i) for i in devices if i - distance in devices]
    return lax.ppermute(block, axis, route)


def head_norm(raw_vals):
    factor = lax.rsqrt(jnp.mean(raw_vals * raw_vals, axis=-1, keepdims=True) + norm_eps)
    return (raw_vals * factor, factor)


def norm_back(raw_vals, factor, grad_in):
    inner_mean = jnp.mean(raw_vals * grad_in, axis=-1, keepdims=True)
    return factor * grad_in - raw_vals * factor * factor * factor * inner_mean


def dot_nt(a, b):
    return lax.dot_general(a, b, (((1,), (1,)), ((), ())), preferred_element_type=jnp.float32)


def dot_nn(a, b):
    return jnp.dot(a, b, preferred_element_type=jnp.float32)


def attention_kernel(halo_span, start_ref, qkv_ref, *refs):
    kv_refs = refs[: halo_span + 1]
    go_ref, out_ref, gq_ref, own_ref = refs[halo_span + 1 : halo_span + 5]
    back_refs = refs[halo_span + 5 : 2 * halo_span + 5]
    kv, kv_t, acc, e_buf = refs[2 * halo_span + 5 :]
    rows = qkv_ref.shape[0]
    d = HEAD_DIM
    for n, ref in enumerate(kv_refs):
        block = ref[...]
        kv[n * rows : (n + 1) * rows, :] = block
        kv_t[:, n * rows : (n + 1) * rows] = jnp.transpose(block.astype(jnp.float32)).astype(
            jnp.bfloat16
        )
    acc[...] = jnp.zeros_like(acc)
    chunks = ATTEND_SPAN // TILE + 1
    heads = Q_PER_KV
    for t in range(rows // TILE):
        r0 = t * TILE
        q_raw = jnp.concatenate(
            [qkv_ref[r0 : r0 + TILE, h * d : (h + 1) * d] for h in range(heads)], 0
        )
        q_unit, q_factor = head_norm(q_raw)
        q16 = q_unit.astype(jnp.bfloat16)
        go = jnp.concatenate([go_ref[r0 : r0 + TILE, h * d : (h + 1) * d] for h in range(heads)], 0)
        key_row = lax.broadcasted_iota(jnp.int32, (TILE, heads * TILE), 0)
        query_col = lax.broadcasted_iota(jnp.int32, (TILE, heads * TILE), 1) % TILE
        total = jnp.zeros((1, heads * TILE), jnp.float32)
        for c in range(chunks):
            k0 = r0 + c * TILE
            scores = dot_nt(kv[k0 : k0 + TILE, :d], q16)
            e = jnp.exp2(scores * (score_scale * log2_e))
            if c == 0:
                e = jnp.where(key_row > query_col, e, 0.0)
            if c == chunks - 1:
                e = jnp.where(key_row <= query_col, e, 0.0)
            if k0 < ATTEND_SPAN:
                e = e * jnp.where(start_ref[0] + k0 >= 0, 1.0, 0.0)
            total = total + jnp.sum(e, axis=0, keepdims=True)
            e_buf[c * TILE : (c + 1) * TILE, :] = e
        inverse = 1.0 / total
        mixed_t = jnp.zeros((d, heads * TILE), jnp.float32)
        for c in range(chunks):
            k0 = r0 + c * TILE
            p = e_buf[c * TILE : (c + 1) * TILE, :] * inverse
            e_buf[c * TILE : (c + 1) * TILE, :] = p
            mixed_t = mixed_t + dot_nn(kv_t[d:, k0 : k0 + TILE], p.astype(jnp.bfloat16))
        go_t = jnp.transpose(go.astype(jnp.float32))
        delta = jnp.sum(go_t * mixed_t, axis=0, keepdims=True)
        mixed = jnp.transpose(mixed_t).astype(jnp.bfloat16)
        for h in range(heads):
            out_ref[r0 : r0 + TILE, h * d : (h + 1) * d] = mixed[h * TILE : (h + 1) * TILE]
        gq_t = jnp.zeros((d, heads * TILE), jnp.float32)
        for c in range(chunks):
            k0 = r0 + c * TILE
            p = e_buf[c * TILE : (c + 1) * TILE, :]
            grad_p = dot_nt(kv[k0 : k0 + TILE, d:], go)
            grad_s = (p * (grad_p - delta)).astype(jnp.bfloat16)
            gq_t = gq_t + dot_nn(kv_t[:d, k0 : k0 + TILE], grad_s)
            acc[k0 : k0 + TILE, :d] += dot_nn(grad_s, q16)
            acc[k0 : k0 + TILE, d:] += dot_nn(p.astype(jnp.bfloat16), go)
        gq = jnp.transpose(gq_t) * score_scale
        gq_raw = norm_back(q_raw, q_factor, gq).astype(jnp.bfloat16)
        for h in range(heads):
            gq_ref[r0 : r0 + TILE, h * d : (h + 1) * d] = gq_raw[h * TILE : (h + 1) * TILE]
    own0 = halo_span * rows
    own_ref[:, :d] = acc[own0:, :d] * score_scale
    own_ref[:, d:] = acc[own0:, d:]
    for n, ref in enumerate(back_refs):
        low = (halo_span - 1 - n) * rows
        ref[:, :d] = (acc[low : low + rows, :d] * score_scale).astype(jnp.bfloat16)
        ref[:, d:] = acc[low : low + rows, d:].astype(jnp.bfloat16)


def group_attention(qkv, kv_list, grad_out, key_start):
    rows = qkv.shape[0]
    halo_span = len(kv_list) - 1
    d = HEAD_DIM
    q_cols = Q_PER_KV * d
    ext = (halo_span + 1) * rows
    window = ATTEND_SPAN + TILE
    elems = Q_PER_KV * rows * window
    vmem = pl.BlockSpec(memory_space=pltpu.VMEM)
    return pl.pallas_call(
        functools.partial(attention_kernel, halo_span),
        out_shape=(
            jax.ShapeDtypeStruct((rows, q_cols), jnp.bfloat16),
            jax.ShapeDtypeStruct((rows, q_cols), jnp.bfloat16),
            jax.ShapeDtypeStruct((rows, 2 * d), jnp.float32),
        )
        + (jax.ShapeDtypeStruct((rows, 2 * d), jnp.bfloat16),) * halo_span,
        in_specs=[pl.BlockSpec(memory_space=pltpu.SMEM)] + [vmem] * (halo_span + 3),
        out_specs=(vmem,) * (3 + halo_span),
        scratch_shapes=[
            pltpu.VMEM((ext, 2 * d), jnp.bfloat16),
            pltpu.VMEM((2 * d, ext), jnp.bfloat16),
            pltpu.VMEM((ext, 2 * d), jnp.float32),
            pltpu.VMEM((window, Q_PER_KV * TILE), jnp.float32),
        ],
        cost_estimate=pl.CostEstimate(
            flops=10 * elems * d, bytes_accessed=6 * rows * 1024, transcendentals=elems
        ),
        compiler_params=pltpu.CompilerParams(vmem_limit_bytes=32 * 1024 * 1024),
    )(key_start, qkv, *kv_list, grad_out)


def per_device(normed, cotangent, qkv_master, adam_first, adam_second, skip_flag, scale_exponent):
    tok_rows = normed.shape[0]
    kv_groups = qkv_master.shape[1]
    d = HEAD_DIM
    q_cols = Q_PER_KV * d
    halo_span = ATTEND_SPAN // tok_rows
    head_count = lax.axis_size("head")
    head_pos = lax.axis_index("head")
    part_rows = tok_rows // head_count
    key_start = (lax.axis_index("seq") * tok_rows - halo_span * tok_rows).astype(jnp.int32)
    key_start = key_start.reshape(1)
    scale_power = jnp.left_shift(jnp.int32(1), scale_exponent[0]).astype(jnp.float32)
    grad_out = (cotangent.astype(jnp.float32) * scale_power).astype(jnp.bfloat16)

    weights = [
        lax.all_gather(qkv_master[:, g, :].astype(jnp.bfloat16), "seq", axis=0, tiled=True)
        for g in range(kv_groups)
    ]
    outs, sums = [], []
    own_part = peer_part = None
    for g in range(kv_groups):
        qkv = dot_nn(normed, weights[g])
        k_raw = qkv[:, q_cols : q_cols + d]
        k_unit, k_factor = head_norm(k_raw)
        kv = jnp.concatenate([k_unit, qkv[:, q_cols + d :]], 1).astype(jnp.bfloat16)
        kv_list = [shifted(kv, "seq", s) for s in range(halo_span, 0, -1)] + [kv]
        out, gq, own, *backs = group_attention(
            qkv, kv_list, grad_out[:, g * q_cols : (g + 1) * q_cols], key_start
        )
        outs.append(out)
        for s in range(1, halo_span + 1):
            own = own + shifted(backs[s - 1], "seq", -s).astype(jnp.float32)
        gk = norm_back(k_raw, k_factor, own[:, :d])
        grad_qkv = jnp.concatenate([gq, gk.astype(jnp.bfloat16), own[:, d:].astype(jnp.bfloat16)], 1)
        term = lax.dot_general(
            normed, grad_qkv, (((0,), (0,)), ((), ())), preferred_element_type=jnp.float32
        )
        sums.append(
            lax.psum_scatter(
                term.astype(jnp.bfloat16), "seq", scatter_dimension=0, tiled=True
            ).astype(jnp.float32)
        )
        if head_count == 2:
            peer_rows = lax.dynamic_slice_in_dim(grad_qkv, (1 - head_pos) * part_rows, part_rows, 0)
            own_rows = lax.dynamic_slice_in_dim(grad_qkv, head_pos * part_rows, part_rows, 0)
            peer_term = dot_nt(peer_rows, weights[g])
            peer_part = peer_term if peer_part is None else peer_part + peer_term
        else:
            own_rows = grad_qkv
        own_term = dot_nt(own_rows, weights[g])
        own_part = own_term if own_part is None else own_part + own_term
    if head_count == 2:
        far_part = lax.ppermute(peer_part.astype(jnp.bfloat16), "head", [(0, 1), (1, 0)])
        d_tokens = own_part + far_part.astype(jnp.float32)
    else:
        d_tokens = lax.psum_scatter(own_part, "head", scatter_dimension=0, tiled=True)
    d_tokens = d_tokens.astype(jnp.bfloat16)
    attn_out = jnp.concatenate(outs, 1)
    gradient = jnp.stack(sums, 1) / scale_power
    first_new = beta_one * adam_first + (1.0 - beta_one) * gradient
    second_new = beta_two * adam_second + (1.0 - beta_two) * gradient * gradient
    first_fix = 1.0 - beta_one**ADAM_STEP
    second_fix = 1.0 - beta_two**ADAM_STEP
    update = first_new / first_fix / (jnp.sqrt(second_new / second_fix) + adam_eps)
    master_new = qkv_master - learn_rate * (update + weight_decay * qkv_master)
    own_flags = lax.dynamic_slice_in_dim(skip_flag, head_pos * kv_groups, kv_groups, 0)
    applied = (own_flags == 0)[None, :, None]
    return (
        attn_out,
        d_tokens,
        jnp.where(applied, master_new, qkv_master),
        jnp.where(applied, first_new, adam_first),
        jnp.where(applied, second_new, adam_second),
    )


def solution(mesh):
    return jax.shard_map(
        per_device,
        mesh=mesh,
        in_specs=(
            P("seq", None),
            P("seq", "head"),
            P("seq", "head", None),
            P("seq", "head", None),
            P("seq", "head", None),
            P(),
            P(),
        ),
        out_specs=(
            P("seq", "head"),
            P(("seq", "head"), None),
            P("seq", "head", None),
            P("seq", "head", None),
            P("seq", "head", None),
        ),
        check_vma=False,
    )
```

```python
import functools

import jax
import jax.numpy as jnp
from jax import lax
from jax.experimental import pallas as pl
from jax.experimental.pallas import tpu as pltpu
from jax.sharding import PartitionSpec as P

HEAD_DIM = 128
ATTEND_SPAN = 1024
ATTN_SCALAR = 168
Q_PER_KV = 2
ADAM_STEP = 1000
TILE = 128


norm_eps = 1e-06
beta_one = 0.9
beta_two = 0.95
adam_eps = 1e-08
learn_rate = 0.01
weight_decay = 0.1
score_scale = float(ATTN_SCALAR) ** (-0.5)
log2_e = 1.4426950408889634


def shifted(block, axis, distance):
    devices = range(lax.axis_size(axis))
    route = [(i - distance, i) for i in devices if i - distance in devices]
    return lax.ppermute(block, axis, route)


def head_norm(raw_vals):
    factor = lax.rsqrt(jnp.mean(raw_vals * raw_vals, axis=-1, keepdims=True) + norm_eps)
    return (raw_vals * factor, factor)


def norm_back(raw_vals, factor, grad_in):
    inner_mean = jnp.mean(raw_vals * grad_in, axis=-1, keepdims=True)
    return factor * grad_in - raw_vals * factor * factor * factor * inner_mean


def dot_nt(a, b):
    return lax.dot_general(a, b, (((1,), (1,)), ((), ())), preferred_element_type=jnp.float32)


def dot_nn(a, b):
    return jnp.dot(a, b, preferred_element_type=jnp.float32)


def attention_kernel(halo_span, start_ref, qkv_ref, *refs):
    kv_refs = refs[: halo_span + 1]
    go_ref, out_ref, gq_ref, own_ref = refs[halo_span + 1 : halo_span + 5]
    back_refs = refs[halo_span + 5 : 2 * halo_span + 5]
    kv, kv_t, acc, e_buf = refs[2 * halo_span + 5 :]
    rows = qkv_ref.shape[0]
    d = HEAD_DIM
    for n, ref in enumerate(kv_refs):
        block = ref[...]
        kv[n * rows : (n + 1) * rows, :] = block
        kv_t[:, n * rows : (n + 1) * rows] = jnp.transpose(block.astype(jnp.float32)).astype(
            jnp.bfloat16
        )
    acc[...] = jnp.zeros_like(acc)
    chunks = ATTEND_SPAN // TILE + 1
    heads = Q_PER_KV
    for t in range(rows // TILE):
        r0 = t * TILE
        q_raw = jnp.concatenate(
            [qkv_ref[r0 : r0 + TILE, h * d : (h + 1) * d] for h in range(heads)], 0
        )
        q_unit, q_factor = head_norm(q_raw)
        q16 = q_unit.astype(jnp.bfloat16)
        go = jnp.concatenate([go_ref[r0 : r0 + TILE, h * d : (h + 1) * d] for h in range(heads)], 0)
        key_row = lax.broadcasted_iota(jnp.int32, (TILE, heads * TILE), 0)
        query_col = lax.broadcasted_iota(jnp.int32, (TILE, heads * TILE), 1) % TILE
        total = jnp.zeros((1, heads * TILE), jnp.float32)
        for c in range(chunks):
            k0 = r0 + c * TILE
            scores = dot_nt(kv[k0 : k0 + TILE, :d], q16)
            e = jnp.exp2(scores * (score_scale * log2_e))
            if c == 0:
                e = jnp.where(key_row > query_col, e, 0.0)
            if c == chunks - 1:
                e = jnp.where(key_row <= query_col, e, 0.0)
            if k0 < ATTEND_SPAN:
                e = e * jnp.where(start_ref[0] + k0 >= 0, 1.0, 0.0)
            total = total + jnp.sum(e, axis=0, keepdims=True)
            e_buf[c * TILE : (c + 1) * TILE, :] = e
        inverse = 1.0 / total
        mixed_t = jnp.zeros((d, heads * TILE), jnp.float32)
        for c in range(chunks):
            k0 = r0 + c * TILE
            p = e_buf[c * TILE : (c + 1) * TILE, :] * inverse
            e_buf[c * TILE : (c + 1) * TILE, :] = p
            mixed_t = mixed_t + dot_nn(kv_t[d:, k0 : k0 + TILE], p.astype(jnp.bfloat16))
        go_t = jnp.transpose(go.astype(jnp.float32))
        delta = jnp.sum(go_t * mixed_t, axis=0, keepdims=True)
        mixed = jnp.transpose(mixed_t).astype(jnp.bfloat16)
        for h in range(heads):
            out_ref[r0 : r0 + TILE, h * d : (h + 1) * d] = mixed[h * TILE : (h + 1) * TILE]
        gq_t = jnp.zeros((d, heads * TILE), jnp.float32)
        for c in range(chunks):
            k0 = r0 + c * TILE
            p = e_buf[c * TILE : (c + 1) * TILE, :]
            grad_p = dot_nt(kv[k0 : k0 + TILE, d:], go)
            grad_s = (p * (grad_p - delta)).astype(jnp.bfloat16)
            gq_t = gq_t + dot_nn(kv_t[:d, k0 : k0 + TILE], grad_s)
            acc[k0 : k0 + TILE, :d] += dot_nn(grad_s, q16)
            acc[k0 : k0 + TILE, d:] += dot_nn(p.astype(jnp.bfloat16), go)
        gq = jnp.transpose(gq_t) * score_scale
        gq_raw = norm_back(q_raw, q_factor, gq).astype(jnp.bfloat16)
        for h in range(heads):
            gq_ref[r0 : r0 + TILE, h * d : (h + 1) * d] = gq_raw[h * TILE : (h + 1) * TILE]
    own0 = halo_span * rows
    own_ref[:, :d] = acc[own0:, :d] * score_scale
    own_ref[:, d:] = acc[own0:, d:]
    for n, ref in enumerate(back_refs):
        low = (halo_span - 1 - n) * rows
        ref[:, :d] = (acc[low : low + rows, :d] * score_scale).astype(jnp.bfloat16)
        ref[:, d:] = acc[low : low + rows, d:].astype(jnp.bfloat16)


def group_attention(qkv, kv_list, grad_out, key_start):
    rows = qkv.shape[0]
    halo_span = len(kv_list) - 1
    d = HEAD_DIM
    q_cols = Q_PER_KV * d
    groups = grad_out.shape[1] // q_cols
    ext = (halo_span + 1) * rows
    window = ATTEND_SPAN + TILE
    elems = groups * Q_PER_KV * rows * window

    def block(cols):
        return pl.BlockSpec((rows, cols), lambda g: (0, g))

    def result(cols, kind):
        return jax.ShapeDtypeStruct((rows, groups * cols), kind)

    return pl.pallas_call(
        functools.partial(attention_kernel, halo_span),
        grid=(groups,),
        out_shape=(
            result(q_cols, jnp.bfloat16),
            result(q_cols, jnp.bfloat16),
            result(2 * d, jnp.float32),
        )
        + (result(2 * d, jnp.bfloat16),) * halo_span,
        in_specs=[pl.BlockSpec(memory_space=pltpu.SMEM), block(q_cols + 2 * d)]
        + [block(2 * d)] * (halo_span + 1)
        + [block(q_cols)],
        out_specs=(block(q_cols), block(q_cols), block(2 * d)) + (block(2 * d),) * halo_span,
        scratch_shapes=[
            pltpu.VMEM((ext, 2 * d), jnp.bfloat16),
            pltpu.VMEM((2 * d, ext), jnp.bfloat16),
            pltpu.VMEM((ext, 2 * d), jnp.float32),
            pltpu.VMEM((window, Q_PER_KV * TILE), jnp.float32),
        ],
        cost_estimate=pl.CostEstimate(
            flops=10 * elems * d,
            bytes_accessed=groups * 6 * rows * 1024,
            transcendentals=elems,
        ),
        compiler_params=pltpu.CompilerParams(vmem_limit_bytes=32 * 1024 * 1024),
    )(key_start, qkv, *kv_list, grad_out)


def row_blocks(normed, own_rows):
    seq_size = lax.axis_size("seq")
    seq_pos = lax.axis_index("seq")
    core, mid = seq_pos % 2, (seq_pos // 2) % 2
    outer = seq_size // 4
    rows = normed.T.reshape(outer, 2, 2, own_rows, normed.shape[0])

    def pick(mid_at, core_at):
        part = lax.dynamic_index_in_dim(rows, core_at, 2, keepdims=False)
        part = lax.dynamic_index_in_dim(part, mid_at, 1, keepdims=False)
        return part.reshape(outer * own_rows, normed.shape[0])

    other_core = jnp.concatenate([pick(1 - mid, 1 - core), pick(mid, 1 - core)], 0)
    return other_core, pick(1 - mid, core), pick(mid, core)


def reduce_rows(blocks, grad_qkv):
    other_core, other_chip, here = blocks
    seq_size = lax.axis_size("seq")
    outer_pos = lax.axis_index("seq") // 4
    outer = seq_size // 4
    devices = range(seq_size)
    half = here.shape[0]
    sent = dot_nn(other_core, grad_qkv).astype(jnp.bfloat16)
    got = lax.ppermute(sent, "seq", [(i, i ^ 1) for i in devices])
    sent = (dot_nn(other_chip, grad_qkv) + got[:half].astype(jnp.float32)).astype(jnp.bfloat16)
    got_chip = lax.ppermute(sent, "seq", [(i, i ^ 2) for i in devices])
    total = (
        dot_nn(here, grad_qkv) + got[half:].astype(jnp.float32) + got_chip.astype(jnp.float32)
    ).astype(jnp.bfloat16)
    total = total.reshape(outer, half // outer, grad_qkv.shape[1])

    def part(at):
        return lax.dynamic_index_in_dim(total, at, 0, keepdims=False)

    parts = [part(outer_pos)]
    for step in range(1, outer):
        route = [(i, (i + 4 * step) % seq_size) for i in devices]
        got = lax.ppermute(part((outer_pos + step) % outer), "seq", route)
        parts.append(got)
    return total, parts


def adam_kernel(part_count, flag_ref, scale_ref, *refs):
    groups = flag_ref.shape[0]
    part_refs = refs[: groups * part_count]
    master_ref, first_ref, second_ref, *out_refs = refs[groups * part_count :]
    first_fix = 1.0 - beta_one**ADAM_STEP
    second_fix = 1.0 - beta_two**ADAM_STEP
    for g in range(groups):
        gradient = part_refs[g * part_count][...].astype(jnp.float32)
        for ref in part_refs[g * part_count + 1 : (g + 1) * part_count]:
            gradient = gradient + ref[...].astype(jnp.float32)
        gradient = gradient * scale_ref[0]
        master, first, second = master_ref[:, g, :], first_ref[:, g, :], second_ref[:, g, :]
        first_new = beta_one * first + (1.0 - beta_one) * gradient
        second_new = beta_two * second + (1.0 - beta_two) * gradient * gradient
        update = first_new / first_fix / (jnp.sqrt(second_new / second_fix) + adam_eps)
        master_new = master - learn_rate * (update + weight_decay * master)
        applied = flag_ref[g] == 0
        for ref, new, old in zip(
            out_refs, (master_new, first_new, second_new), (master, first, second)
        ):
            ref[:, g, :] = jnp.where(applied, new, old)


def adam_step(own_flags, inverse_scale, sums, *state):
    own_rows, groups, cols = state[0].shape
    part_count = len(sums[0])
    rows = own_rows
    for size in (112, 56, 48):
        if own_rows % size == 0:
            rows = size
            break
    smem = pl.BlockSpec(memory_space=pltpu.SMEM)
    part = pl.BlockSpec((rows, cols), lambda i: (i, 0))
    whole = pl.BlockSpec((rows, groups, cols), lambda i: (i, 0, 0))
    return pl.pallas_call(
        functools.partial(adam_kernel, part_count),
        grid=(own_rows // rows,),
        out_shape=(jax.ShapeDtypeStruct(state[0].shape, jnp.float32),) * 3,
        in_specs=[smem, smem] + [part] * (groups * part_count) + [whole] * 3,
        out_specs=(whole,) * 3,
        cost_estimate=pl.CostEstimate(
            flops=20 * state[0].size, bytes_accessed=32 * state[0].size, transcendentals=0
        ),
        compiler_params=pltpu.CompilerParams(vmem_limit_bytes=40 * 1024 * 1024),
    )(own_flags, inverse_scale, *[p for parts in sums for p in parts], *state)


def per_device(normed, cotangent, qkv_master, adam_first, adam_second, skip_flag, scale_exponent):
    tok_rows = normed.shape[0]
    own_rows, kv_groups, group_cols = qkv_master.shape
    d = HEAD_DIM
    q_cols = Q_PER_KV * d
    halo_span = ATTEND_SPAN // tok_rows
    head_count = lax.axis_size("head")
    head_pos = lax.axis_index("head")
    part_rows = tok_rows // head_count
    key_start = (lax.axis_index("seq") * tok_rows - halo_span * tok_rows).astype(jnp.int32)
    key_start = key_start.reshape(1)
    scale_power = jnp.left_shift(jnp.int32(1), scale_exponent[0]).astype(jnp.float32)
    grad_out = (cotangent.astype(jnp.float32) * scale_power).astype(jnp.bfloat16)

    master16 = qkv_master.astype(jnp.bfloat16).reshape(own_rows, kv_groups * group_cols)
    weights = lax.all_gather(master16, "seq", axis=0, tiled=True)
    blocks = row_blocks(normed, own_rows)
    pair = 2 if kv_groups % 2 == 0 else 1
    outs, grads, sums = [], [], []
    for low in range(0, kv_groups, pair):
        qkv = dot_nn(normed, weights[:, low * group_cols : (low + pair) * group_cols])
        kv, k_saved = [], []
        for g in range(pair):
            at = g * group_cols + q_cols
            k_raw = qkv[:, at : at + d]
            k_unit, k_factor = head_norm(k_raw)
            k_saved.append((k_raw, k_factor))
            kv += [k_unit.astype(jnp.bfloat16), qkv[:, at + d : at + 2 * d].astype(jnp.bfloat16)]
        kv = jnp.concatenate(kv, 1)
        kv_list = [shifted(kv, "seq", s) for s in range(halo_span, 0, -1)] + [kv]
        out, gq, own, *backs = group_attention(
            qkv, kv_list, grad_out[:, low * q_cols : (low + pair) * q_cols], key_start
        )
        outs.append(out)
        for s in range(1, halo_span + 1):
            own = own + shifted(backs[s - 1], "seq", -s).astype(jnp.float32)
        for g in range(pair):
            at = g * 2 * d
            gk = norm_back(*k_saved[g], own[:, at : at + d])
            grad_qkv = jnp.concatenate(
                [
                    gq[:, g * q_cols : (g + 1) * q_cols],
                    gk.astype(jnp.bfloat16),
                    own[:, at + d : at + 2 * d].astype(jnp.bfloat16),
                ],
                1,
            )
            grad_qkv = lax.optimization_barrier(grad_qkv)
            grads.append(grad_qkv)
            total, parts = reduce_rows(blocks, grad_qkv)
            sums.append(parts)
    grad_qkv = jnp.concatenate(grads, 1)
    if head_count == 2:
        peer_rows = lax.dynamic_slice_in_dim(grad_qkv, (1 - head_pos) * part_rows, part_rows, 0)
        far_part = lax.ppermute(
            dot_nt(peer_rows, weights).astype(jnp.bfloat16), "head", [(0, 1), (1, 0)]
        )
        far_part, _ = lax.optimization_barrier((far_part, total))
        mine = lax.dynamic_slice_in_dim(grad_qkv, head_pos * part_rows, part_rows, 0)
        d_tokens = dot_nt(mine, weights) + far_part.astype(jnp.float32)
    else:
        d_tokens = lax.psum_scatter(
            dot_nt(grad_qkv, weights), "head", scatter_dimension=0, tiled=True
        )
    d_tokens = d_tokens.astype(jnp.bfloat16)
    attn_out = jnp.concatenate(outs, 1)
    own_flags = lax.dynamic_slice_in_dim(skip_flag, head_pos * kv_groups, kv_groups, 0)
    stepped = adam_step(
        own_flags, (1.0 / scale_power).reshape(1), sums, qkv_master, adam_first, adam_second
    )
    return (attn_out, d_tokens, *stepped)


def solution(mesh):
    return jax.shard_map(
        per_device,
        mesh=mesh,
        in_specs=(
            P("seq", None),
            P("seq", "head"),
            P("seq", "head", None),
            P("seq", "head", None),
            P("seq", "head", None),
            P(),
            P(),
        ),
        out_specs=(
            P("seq", "head"),
            P(("seq", "head"), None),
            P("seq", "head", None),
            P("seq", "head", None),
            P("seq", "head", None),
        ),
        check_vma=False,
    )
```

```python
import functools

import jax
import jax.numpy as jnp
from jax import lax
from jax.experimental import pallas as pl
from jax.experimental.pallas import tpu as pltpu
from jax.sharding import PartitionSpec as P

HEAD_DIM = 128
ATTEND_SPAN = 1024
ATTN_SCALAR = 168
Q_PER_KV = 2
ADAM_STEP = 1000
TILE = 128


norm_eps = 1e-06
beta_one = 0.9
beta_two = 0.95
adam_eps = 1e-08
learn_rate = 0.01
weight_decay = 0.1
score_scale = float(ATTN_SCALAR) ** (-0.5)
log2_e = 1.4426950408889634


def shifted(block, axis, distance):
    devices = range(lax.axis_size(axis))
    route = [(i - distance, i) for i in devices if i - distance in devices]
    return lax.ppermute(block, axis, route)


def head_norm(raw_vals):
    factor = lax.rsqrt(jnp.mean(raw_vals * raw_vals, axis=-1, keepdims=True) + norm_eps)
    return (raw_vals * factor, factor)


def norm_back(raw_vals, factor, grad_in):
    inner_mean = jnp.mean(raw_vals * grad_in, axis=-1, keepdims=True)
    return factor * grad_in - raw_vals * factor * factor * factor * inner_mean


def dot_nt(a, b):
    return lax.dot_general(a, b, (((1,), (1,)), ((), ())), preferred_element_type=jnp.float32)


def dot_nn(a, b):
    return jnp.dot(a, b, preferred_element_type=jnp.float32)


def attention_kernel(halo_span, start_ref, qkv_ref, *refs):
    kv_refs = refs[: halo_span + 1]
    go_ref, out_ref, gq_ref, own_ref = refs[halo_span + 1 : halo_span + 5]
    back_refs = refs[halo_span + 5 : 2 * halo_span + 5]
    kv, kv_t, acc, e_buf = refs[2 * halo_span + 5 :]
    rows = qkv_ref.shape[0]
    d = HEAD_DIM
    for n, ref in enumerate(kv_refs):
        block = ref[...]
        kv[n * rows : (n + 1) * rows, :] = block
        kv_t[:, n * rows : (n + 1) * rows] = jnp.transpose(block.astype(jnp.float32)).astype(
            jnp.bfloat16
        )
    acc[...] = jnp.zeros_like(acc)
    chunks = ATTEND_SPAN // TILE + 1
    heads = Q_PER_KV
    for t in range(rows // TILE):
        r0 = t * TILE
        q_raw = jnp.concatenate(
            [qkv_ref[r0 : r0 + TILE, h * d : (h + 1) * d] for h in range(heads)], 0
        )
        q_unit, q_factor = head_norm(q_raw)
        q16 = q_unit.astype(jnp.bfloat16)
        go = jnp.concatenate([go_ref[r0 : r0 + TILE, h * d : (h + 1) * d] for h in range(heads)], 0)
        key_row = lax.broadcasted_iota(jnp.int32, (TILE, heads * TILE), 0)
        query_col = lax.broadcasted_iota(jnp.int32, (TILE, heads * TILE), 1) % TILE
        total = jnp.zeros((1, heads * TILE), jnp.float32)
        for c in range(chunks):
            k0 = r0 + c * TILE
            scores = dot_nt(kv[k0 : k0 + TILE, :d], q16)
            e = jnp.exp2(scores * (score_scale * log2_e))
            if c == 0:
                e = jnp.where(key_row > query_col, e, 0.0)
            if c == chunks - 1:
                e = jnp.where(key_row <= query_col, e, 0.0)
            if k0 < ATTEND_SPAN:
                e = e * jnp.where(start_ref[0] + k0 >= 0, 1.0, 0.0)
            total = total + jnp.sum(e, axis=0, keepdims=True)
            e_buf[c * TILE : (c + 1) * TILE, :] = e
        inverse = 1.0 / total
        mixed_t = jnp.zeros((d, heads * TILE), jnp.float32)
        for c in range(chunks):
            k0 = r0 + c * TILE
            p = e_buf[c * TILE : (c + 1) * TILE, :] * inverse
            e_buf[c * TILE : (c + 1) * TILE, :] = p
            mixed_t = mixed_t + dot_nn(kv_t[d:, k0 : k0 + TILE], p.astype(jnp.bfloat16))
        go_t = jnp.transpose(go.astype(jnp.float32))
        delta = jnp.sum(go_t * mixed_t, axis=0, keepdims=True)
        mixed = jnp.transpose(mixed_t).astype(jnp.bfloat16)
        for h in range(heads):
            out_ref[r0 : r0 + TILE, h * d : (h + 1) * d] = mixed[h * TILE : (h + 1) * TILE]
        gq_t = jnp.zeros((d, heads * TILE), jnp.float32)
        for c in range(chunks):
            k0 = r0 + c * TILE
            p = e_buf[c * TILE : (c + 1) * TILE, :]
            grad_p = dot_nt(kv[k0 : k0 + TILE, d:], go)
            grad_s = (p * (grad_p - delta)).astype(jnp.bfloat16)
            gq_t = gq_t + dot_nn(kv_t[:d, k0 : k0 + TILE], grad_s)
            acc[k0 : k0 + TILE, :d] += dot_nn(grad_s, q16)
            acc[k0 : k0 + TILE, d:] += dot_nn(p.astype(jnp.bfloat16), go)
        gq = jnp.transpose(gq_t) * score_scale
        gq_raw = norm_back(q_raw, q_factor, gq).astype(jnp.bfloat16)
        for h in range(heads):
            gq_ref[r0 : r0 + TILE, h * d : (h + 1) * d] = gq_raw[h * TILE : (h + 1) * TILE]
    own0 = halo_span * rows
    own_ref[:, :d] = acc[own0:, :d] * score_scale
    own_ref[:, d:] = acc[own0:, d:]
    for n, ref in enumerate(back_refs):
        low = (halo_span - 1 - n) * rows
        ref[:, :d] = (acc[low : low + rows, :d] * score_scale).astype(jnp.bfloat16)
        ref[:, d:] = acc[low : low + rows, d:].astype(jnp.bfloat16)


def group_attention(qkv, kv_list, grad_out, key_start):
    rows = qkv.shape[0]
    halo_span = len(kv_list) - 1
    d = HEAD_DIM
    q_cols = Q_PER_KV * d
    groups = grad_out.shape[1] // q_cols
    ext = (halo_span + 1) * rows
    window = ATTEND_SPAN + TILE
    elems = groups * Q_PER_KV * rows * window

    def block(cols):
        return pl.BlockSpec((rows, cols), lambda g: (0, g))

    def result(cols, kind):
        return jax.ShapeDtypeStruct((rows, groups * cols), kind)

    return pl.pallas_call(
        functools.partial(attention_kernel, halo_span),
        grid=(groups,),
        out_shape=(
            result(q_cols, jnp.bfloat16),
            result(q_cols, jnp.bfloat16),
            result(2 * d, jnp.float32),
        )
        + (result(2 * d, jnp.bfloat16),) * halo_span,
        in_specs=[pl.BlockSpec(memory_space=pltpu.SMEM), block(q_cols + 2 * d)]
        + [block(2 * d)] * (halo_span + 1)
        + [block(q_cols)],
        out_specs=(block(q_cols), block(q_cols), block(2 * d)) + (block(2 * d),) * halo_span,
        scratch_shapes=[
            pltpu.VMEM((ext, 2 * d), jnp.bfloat16),
            pltpu.VMEM((2 * d, ext), jnp.bfloat16),
            pltpu.VMEM((ext, 2 * d), jnp.float32),
            pltpu.VMEM((window, Q_PER_KV * TILE), jnp.float32),
        ],
        cost_estimate=pl.CostEstimate(
            flops=10 * elems * d,
            bytes_accessed=groups * 6 * rows * 1024,
            transcendentals=elems,
        ),
        compiler_params=pltpu.CompilerParams(vmem_limit_bytes=32 * 1024 * 1024),
    )(key_start, qkv, *kv_list, grad_out)


def row_blocks(normed, own_rows):
    seq_size = lax.axis_size("seq")
    seq_pos = lax.axis_index("seq")
    core, mid = seq_pos % 2, (seq_pos // 2) % 2
    outer = seq_size // 4
    rows = normed.T.reshape(outer, 2, 2, own_rows, normed.shape[0])

    def pick(mid_at, core_at):
        part = lax.dynamic_index_in_dim(rows, core_at, 2, keepdims=False)
        part = lax.dynamic_index_in_dim(part, mid_at, 1, keepdims=False)
        return part.reshape(outer * own_rows, normed.shape[0])

    other_core = jnp.concatenate([pick(1 - mid, 1 - core), pick(mid, 1 - core)], 0)
    return other_core, pick(1 - mid, core), pick(mid, core)


def after(value, *earlier):
    return lax.optimization_barrier((value, *earlier))[0]


def reduce_rows(blocks, grad_qkv, earlier):
    other_core, other_chip, here = blocks
    seq_size = lax.axis_size("seq")
    outer_pos = lax.axis_index("seq") // 4
    outer = seq_size // 4
    devices = range(seq_size)
    half = here.shape[0]
    sent = dot_nn(other_core, grad_qkv).astype(jnp.bfloat16)
    got = lax.ppermute(sent, "seq", [(i, i ^ 1) for i in devices])
    sent = (dot_nn(other_chip, grad_qkv) + got[:half].astype(jnp.float32)).astype(jnp.bfloat16)
    got_chip = lax.ppermute(sent, "seq", [(i, i ^ 2) for i in devices])
    got_chip = after(got_chip, *earlier)
    total = (
        dot_nn(here, grad_qkv) + got[half:].astype(jnp.float32) + got_chip.astype(jnp.float32)
    ).astype(jnp.bfloat16)
    total = total.reshape(outer, half // outer, grad_qkv.shape[1])

    def part(at):
        return lax.dynamic_index_in_dim(total, at, 0, keepdims=False)

    parts = [part(outer_pos)]
    for step in range(1, outer):
        route = [(i, (i + 4 * step) % seq_size) for i in devices]
        got = lax.ppermute(part((outer_pos + step) % outer), "seq", route)
        parts.append(got)
    return sent, total, parts


def adam_kernel(part_count, flag_ref, scale_ref, *refs):
    groups = flag_ref.shape[0]
    part_refs = refs[: groups * part_count]
    master_ref, first_ref, second_ref, *out_refs = refs[groups * part_count :]
    first_fix = 1.0 - beta_one**ADAM_STEP
    second_fix = 1.0 - beta_two**ADAM_STEP
    for g in range(groups):
        gradient = part_refs[g * part_count][...].astype(jnp.float32)
        for ref in part_refs[g * part_count + 1 : (g + 1) * part_count]:
            gradient = gradient + ref[...].astype(jnp.float32)
        gradient = gradient * scale_ref[0]
        master, first, second = master_ref[:, g, :], first_ref[:, g, :], second_ref[:, g, :]
        first_new = beta_one * first + (1.0 - beta_one) * gradient
        second_new = beta_two * second + (1.0 - beta_two) * gradient * gradient
        update = first_new / first_fix / (jnp.sqrt(second_new / second_fix) + adam_eps)
        master_new = master - learn_rate * (update + weight_decay * master)
        applied = flag_ref[g] == 0
        for ref, new, old in zip(
            out_refs, (master_new, first_new, second_new), (master, first, second)
        ):
            ref[:, g, :] = jnp.where(applied, new, old)


def adam_step(own_flags, inverse_scale, sums, *state):
    own_rows, groups, cols = state[0].shape
    part_count = len(sums[0])
    rows = own_rows
    for size in (112, 56, 48):
        if own_rows % size == 0:
            rows = size
            break
    smem = pl.BlockSpec(memory_space=pltpu.SMEM)
    part = pl.BlockSpec((rows, cols), lambda i: (i, 0))
    whole = pl.BlockSpec((rows, groups, cols), lambda i: (i, 0, 0))
    return pl.pallas_call(
        functools.partial(adam_kernel, part_count),
        grid=(own_rows // rows,),
        out_shape=(jax.ShapeDtypeStruct(state[0].shape, jnp.float32),) * 3,
        in_specs=[smem, smem] + [part] * (groups * part_count) + [whole] * 3,
        out_specs=(whole,) * 3,
        cost_estimate=pl.CostEstimate(
            flops=20 * state[0].size, bytes_accessed=32 * state[0].size, transcendentals=0
        ),
        compiler_params=pltpu.CompilerParams(vmem_limit_bytes=40 * 1024 * 1024),
    )(own_flags, inverse_scale, *[p for parts in sums for p in parts], *state)


def per_device(normed, cotangent, qkv_master, adam_first, adam_second, skip_flag, scale_exponent):
    tok_rows = normed.shape[0]
    own_rows, kv_groups, group_cols = qkv_master.shape
    d = HEAD_DIM
    q_cols = Q_PER_KV * d
    halo_span = ATTEND_SPAN // tok_rows
    head_count = lax.axis_size("head")
    head_pos = lax.axis_index("head")
    part_rows = tok_rows // head_count
    key_start = (lax.axis_index("seq") * tok_rows - halo_span * tok_rows).astype(jnp.int32)
    key_start = key_start.reshape(1)
    scale_power = jnp.left_shift(jnp.int32(1), scale_exponent[0]).astype(jnp.float32)
    grad_out = (cotangent.astype(jnp.float32) * scale_power).astype(jnp.bfloat16)

    master16 = qkv_master.astype(jnp.bfloat16).reshape(own_rows, kv_groups * group_cols)
    pair = 2 if kv_groups % 2 == 0 else 1
    pair_cols = pair * group_cols
    weights = [
        lax.all_gather(master16[:, at : at + pair_cols], "seq", axis=0, tiled=True)
        for at in range(0, kv_groups * group_cols, pair_cols)
    ]
    blocks = row_blocks(normed, own_rows)
    outs, grads, sums = [], [], []
    all_sent, totals = [], []
    for low in range(0, kv_groups, pair):
        pair_weights = weights[low // pair]
        if low:
            pair_weights = after(pair_weights, *all_sent)
        qkv = dot_nn(normed, pair_weights)
        kv, k_saved = [], []
        for g in range(pair):
            at = g * group_cols + q_cols
            k_raw = qkv[:, at : at + d]
            k_unit, k_factor = head_norm(k_raw)
            k_saved.append((k_raw, k_factor))
            kv += [k_unit.astype(jnp.bfloat16), qkv[:, at + d : at + 2 * d].astype(jnp.bfloat16)]
        kv = jnp.concatenate(kv, 1)
        kv_list = [shifted(kv, "seq", s) for s in range(halo_span, 0, -1)] + [kv]
        out, gq, own, *backs = group_attention(
            qkv, kv_list, grad_out[:, low * q_cols : (low + pair) * q_cols], key_start
        )
        outs.append(out)
        for s in range(1, halo_span + 1):
            back = shifted(backs[s - 1], "seq", -s)
            if low:
                back = after(back, *totals)
            own = own + back.astype(jnp.float32)
        pair_sent, pair_totals = [], []
        for g in range(pair):
            at = g * 2 * d
            gk = norm_back(*k_saved[g], own[:, at : at + d])
            grad_qkv = jnp.concatenate(
                [
                    gq[:, g * q_cols : (g + 1) * q_cols],
                    gk.astype(jnp.bfloat16),
                    own[:, at + d : at + 2 * d].astype(jnp.bfloat16),
                ],
                1,
            )
            grad_qkv = lax.optimization_barrier(grad_qkv)
            grads.append(grad_qkv)
            earlier = sums[-2] if len(sums) >= 2 else ()
            sent, total, parts = reduce_rows(blocks, grad_qkv, earlier)
            pair_sent.append(sent)
            pair_totals.append(total)
            sums.append(parts)
        all_sent, totals = all_sent + pair_sent, totals + pair_totals

    def token_terms(rows_at, row_count, *earlier):
        terms = 0.0
        for low in range(0, kv_groups, pair):
            rows = jnp.concatenate(grads[low : low + pair], 1)
            rows = lax.dynamic_slice_in_dim(after(rows, *earlier), rows_at, row_count, 0)
            terms = terms + dot_nt(rows, weights[low // pair])
        return terms

    if head_count == 2:
        peer_terms = token_terms((1 - head_pos) * part_rows, part_rows, *all_sent)
        far_part = lax.ppermute(peer_terms.astype(jnp.bfloat16), "head", [(0, 1), (1, 0)])
        far_part = after(far_part, total)
        d_tokens = token_terms(head_pos * part_rows, part_rows, total)
        d_tokens = d_tokens + far_part.astype(jnp.float32)
    else:
        d_tokens = lax.psum_scatter(
            token_terms(0, tok_rows), "head", scatter_dimension=0, tiled=True
        )
    d_tokens = d_tokens.astype(jnp.bfloat16)
    attn_out = jnp.concatenate(outs, 1)
    own_flags = lax.dynamic_slice_in_dim(skip_flag, head_pos * kv_groups, kv_groups, 0)
    stepped = adam_step(
        own_flags, (1.0 / scale_power).reshape(1), sums, qkv_master, adam_first, adam_second
    )
    return (attn_out, d_tokens, *stepped)


def solution(mesh):
    return jax.shard_map(
        per_device,
        mesh=mesh,
        in_specs=(
            P("seq", None),
            P("seq", "head"),
            P("seq", "head", None),
            P("seq", "head", None),
            P("seq", "head", None),
            P(),
            P(),
        ),
        out_specs=(
            P("seq", "head"),
            P(("seq", "head"), None),
            P("seq", "head", None),
            P("seq", "head", None),
            P("seq", "head", None),
        ),
        check_vma=False,
    )
```

```python
import functools

import jax
import jax.numpy as jnp
from jax import lax
from jax.experimental import pallas as pl
from jax.experimental.pallas import tpu as pltpu
from jax.sharding import PartitionSpec as P

HEAD_DIM = 128
ATTEND_SPAN = 1024
ATTN_SCALAR = 168
Q_PER_KV = 2
ADAM_STEP = 1000
TILE = 128


norm_eps = 1e-06
beta_one = 0.9
beta_two = 0.95
adam_eps = 1e-08
learn_rate = 0.01
weight_decay = 0.1
score_scale = float(ATTN_SCALAR) ** (-0.5)
log2_e = 1.4426950408889634


def shifted(block, axis, distance):
    devices = range(lax.axis_size(axis))
    route = [(i - distance, i) for i in devices if i - distance in devices]
    return lax.ppermute(block, axis, route)


def head_norm(raw_vals):
    factor = lax.rsqrt(jnp.mean(raw_vals * raw_vals, axis=-1, keepdims=True) + norm_eps)
    return (raw_vals * factor, factor)


def norm_back(raw_vals, factor, grad_in):
    inner_mean = jnp.mean(raw_vals * grad_in, axis=-1, keepdims=True)
    return factor * grad_in - raw_vals * factor * factor * factor * inner_mean


def dot_nt(a, b):
    return lax.dot_general(a, b, (((1,), (1,)), ((), ())), preferred_element_type=jnp.float32)


def dot_nn(a, b):
    return jnp.dot(a, b, preferred_element_type=jnp.float32)


def attention_kernel(halo_span, start_ref, qkv_ref, *refs):
    kv_refs = refs[: halo_span + 1]
    go_ref, out_ref, gq_ref, own_ref = refs[halo_span + 1 : halo_span + 5]
    back_refs = refs[halo_span + 5 : 2 * halo_span + 5]
    kv, kv_t, acc, e_buf = refs[2 * halo_span + 5 :]
    rows = qkv_ref.shape[0]
    d = HEAD_DIM
    for n, ref in enumerate(kv_refs):
        block = ref[...]
        kv[n * rows : (n + 1) * rows, :] = block
        kv_t[:, n * rows : (n + 1) * rows] = jnp.transpose(block.astype(jnp.float32)).astype(
            jnp.bfloat16
        )
    acc[...] = jnp.zeros_like(acc)
    chunks = ATTEND_SPAN // TILE + 1
    heads = Q_PER_KV
    for t in range(rows // TILE):
        r0 = t * TILE
        q_raw = jnp.concatenate(
            [qkv_ref[r0 : r0 + TILE, h * d : (h + 1) * d] for h in range(heads)], 0
        )
        q_unit, q_factor = head_norm(q_raw)
        q16 = q_unit.astype(jnp.bfloat16)
        go = jnp.concatenate([go_ref[r0 : r0 + TILE, h * d : (h + 1) * d] for h in range(heads)], 0)
        key_row = lax.broadcasted_iota(jnp.int32, (TILE, heads * TILE), 0)
        query_col = lax.broadcasted_iota(jnp.int32, (TILE, heads * TILE), 1) % TILE
        total = jnp.zeros((1, heads * TILE), jnp.float32)
        for c in range(chunks):
            k0 = r0 + c * TILE
            scores = dot_nt(kv[k0 : k0 + TILE, :d], q16)
            e = jnp.exp2(scores * (score_scale * log2_e))
            if c == 0:
                e = jnp.where(key_row > query_col, e, 0.0)
            if c == chunks - 1:
                e = jnp.where(key_row <= query_col, e, 0.0)
            if k0 < ATTEND_SPAN:
                e = e * jnp.where(start_ref[0] + k0 >= 0, 1.0, 0.0)
            total = total + jnp.sum(e, axis=0, keepdims=True)
            e_buf[c * TILE : (c + 1) * TILE, :] = e
        inverse = 1.0 / total
        mixed_t = jnp.zeros((d, heads * TILE), jnp.float32)
        for c in range(chunks):
            k0 = r0 + c * TILE
            p = e_buf[c * TILE : (c + 1) * TILE, :] * inverse
            e_buf[c * TILE : (c + 1) * TILE, :] = p
            mixed_t = mixed_t + dot_nn(kv_t[d:, k0 : k0 + TILE], p.astype(jnp.bfloat16))
        go_t = jnp.transpose(go.astype(jnp.float32))
        delta = jnp.sum(go_t * mixed_t, axis=0, keepdims=True)
        mixed = jnp.transpose(mixed_t).astype(jnp.bfloat16)
        for h in range(heads):
            out_ref[r0 : r0 + TILE, h * d : (h + 1) * d] = mixed[h * TILE : (h + 1) * TILE]
        gq_t = jnp.zeros((d, heads * TILE), jnp.float32)
        for c in range(chunks):
            k0 = r0 + c * TILE
            p = e_buf[c * TILE : (c + 1) * TILE, :]
            grad_p = dot_nt(kv[k0 : k0 + TILE, d:], go)
            grad_s = (p * (grad_p - delta)).astype(jnp.bfloat16)
            gq_t = gq_t + dot_nn(kv_t[:d, k0 : k0 + TILE], grad_s)
            acc[k0 : k0 + TILE, :d] += dot_nn(grad_s, q16)
            acc[k0 : k0 + TILE, d:] += dot_nn(p.astype(jnp.bfloat16), go)
        gq = jnp.transpose(gq_t) * score_scale
        gq_raw = norm_back(q_raw, q_factor, gq).astype(jnp.bfloat16)
        for h in range(heads):
            gq_ref[r0 : r0 + TILE, h * d : (h + 1) * d] = gq_raw[h * TILE : (h + 1) * TILE]
    own0 = halo_span * rows
    own_ref[:, :d] = acc[own0:, :d] * score_scale
    own_ref[:, d:] = acc[own0:, d:]
    for n, ref in enumerate(back_refs):
        low = (halo_span - 1 - n) * rows
        ref[:, :d] = (acc[low : low + rows, :d] * score_scale).astype(jnp.bfloat16)
        ref[:, d:] = acc[low : low + rows, d:].astype(jnp.bfloat16)


def group_attention(qkv, kv_list, grad_out, key_start, place, grad_place):
    rows = qkv.shape[0]
    halo_span = len(kv_list) - 1
    d = HEAD_DIM
    q_cols = Q_PER_KV * d
    ext = (halo_span + 1) * rows
    window = ATTEND_SPAN + TILE
    elems = Q_PER_KV * rows * window

    def block(cols, at=0):
        return pl.BlockSpec((rows, cols), lambda g: (0, at))

    def result(cols, kind):
        return jax.ShapeDtypeStruct((rows, cols), kind)

    return pl.pallas_call(
        functools.partial(attention_kernel, halo_span),
        grid=(1,),
        out_shape=(
            result(q_cols, jnp.bfloat16),
            result(q_cols, jnp.bfloat16),
            result(2 * d, jnp.float32),
        )
        + (result(2 * d, jnp.bfloat16),) * halo_span,
        in_specs=[pl.BlockSpec(memory_space=pltpu.SMEM), block(q_cols + 2 * d, place)]
        + [block(2 * d, place)] * (halo_span + 1)
        + [block(q_cols, grad_place)],
        out_specs=(block(q_cols), block(q_cols), block(2 * d)) + (block(2 * d),) * halo_span,
        scratch_shapes=[
            pltpu.VMEM((ext, 2 * d), jnp.bfloat16),
            pltpu.VMEM((2 * d, ext), jnp.bfloat16),
            pltpu.VMEM((ext, 2 * d), jnp.float32),
            pltpu.VMEM((window, Q_PER_KV * TILE), jnp.float32),
        ],
        cost_estimate=pl.CostEstimate(
            flops=10 * elems * d,
            bytes_accessed=6 * rows * 1024,
            transcendentals=elems,
        ),
        compiler_params=pltpu.CompilerParams(vmem_limit_bytes=32 * 1024 * 1024),
    )(key_start, qkv, *kv_list, grad_out)


def row_blocks(normed, own_rows):
    seq_size = lax.axis_size("seq")
    seq_pos = lax.axis_index("seq")
    core, mid = seq_pos % 2, (seq_pos // 2) % 2
    outer = seq_size // 4
    rows = normed.T.reshape(outer, 2, 2, own_rows, normed.shape[0])

    def pick(mid_at, core_at):
        part = lax.dynamic_index_in_dim(rows, core_at, 2, keepdims=False)
        part = lax.dynamic_index_in_dim(part, mid_at, 1, keepdims=False)
        return part.reshape(outer * own_rows, normed.shape[0])

    other_core = jnp.concatenate([pick(1 - mid, 1 - core), pick(mid, 1 - core)], 0)
    return other_core, pick(1 - mid, core), pick(mid, core)


def after(value, *earlier):
    return lax.optimization_barrier((value, *earlier))[0]


def reduce_rows(blocks, grad_qkv, earlier):
    other_core, other_chip, here = blocks
    seq_size = lax.axis_size("seq")
    outer_pos = lax.axis_index("seq") // 4
    outer = seq_size // 4
    devices = range(seq_size)
    half = here.shape[0]
    sent = dot_nn(other_core, grad_qkv).astype(jnp.bfloat16)
    got = lax.ppermute(sent, "seq", [(i, i ^ 1) for i in devices])
    sent = (dot_nn(other_chip, grad_qkv) + got[:half].astype(jnp.float32)).astype(jnp.bfloat16)
    got_chip = lax.ppermute(sent, "seq", [(i, i ^ 2) for i in devices])
    got_chip = after(got_chip, *earlier)
    total = (
        dot_nn(here, grad_qkv) + got[half:].astype(jnp.float32) + got_chip.astype(jnp.float32)
    ).astype(jnp.bfloat16)
    total = total.reshape(outer, half // outer, grad_qkv.shape[1])

    def part(at):
        return lax.dynamic_index_in_dim(total, at, 0, keepdims=False)

    parts = [part(outer_pos)]
    for step in range(1, outer):
        route = [(i, (i + 4 * step) % seq_size) for i in devices]
        got = lax.ppermute(part((outer_pos + step) % outer), "seq", route)
        parts.append(got)
    return sent, total, parts


def adam_kernel(part_count, flag_ref, scale_ref, *refs):
    groups = flag_ref.shape[0]
    part_refs = refs[: groups * part_count]
    master_ref, first_ref, second_ref, *out_refs = refs[groups * part_count :]
    first_fix = 1.0 - beta_one**ADAM_STEP
    second_fix = 1.0 - beta_two**ADAM_STEP
    for g in range(groups):
        gradient = part_refs[g * part_count][...].astype(jnp.float32)
        for ref in part_refs[g * part_count + 1 : (g + 1) * part_count]:
            gradient = gradient + ref[...].astype(jnp.float32)
        gradient = gradient * scale_ref[0]
        master, first, second = master_ref[:, g, :], first_ref[:, g, :], second_ref[:, g, :]
        first_new = beta_one * first + (1.0 - beta_one) * gradient
        second_new = beta_two * second + (1.0 - beta_two) * gradient * gradient
        update = first_new / first_fix / (jnp.sqrt(second_new / second_fix) + adam_eps)
        master_new = master - learn_rate * (update + weight_decay * master)
        applied = flag_ref[g] == 0
        for ref, new, old in zip(
            out_refs, (master_new, first_new, second_new), (master, first, second)
        ):
            ref[:, g, :] = jnp.where(applied, new, old)


def adam_step(own_flags, inverse_scale, sums, *state):
    own_rows, groups, cols = state[0].shape
    part_count = len(sums[0])
    rows = own_rows
    for size in (112, 56, 48):
        if own_rows % size == 0:
            rows = size
            break
    smem = pl.BlockSpec(memory_space=pltpu.SMEM)
    part = pl.BlockSpec((rows, cols), lambda i: (i, 0))
    whole = pl.BlockSpec((rows, groups, cols), lambda i: (i, 0, 0))
    return pl.pallas_call(
        functools.partial(adam_kernel, part_count),
        grid=(own_rows // rows,),
        out_shape=(jax.ShapeDtypeStruct(state[0].shape, jnp.float32),) * 3,
        in_specs=[smem, smem] + [part] * (groups * part_count) + [whole] * 3,
        out_specs=(whole,) * 3,
        cost_estimate=pl.CostEstimate(
            flops=20 * state[0].size, bytes_accessed=32 * state[0].size, transcendentals=0
        ),
        compiler_params=pltpu.CompilerParams(vmem_limit_bytes=40 * 1024 * 1024),
    )(own_flags, inverse_scale, *[p for parts in sums for p in parts], *state)


def per_device(normed, cotangent, qkv_master, adam_first, adam_second, skip_flag, scale_exponent):
    tok_rows = normed.shape[0]
    own_rows, kv_groups, group_cols = qkv_master.shape
    d = HEAD_DIM
    q_cols = Q_PER_KV * d
    halo_span = ATTEND_SPAN // tok_rows
    head_count = lax.axis_size("head")
    head_pos = lax.axis_index("head")
    part_rows = tok_rows // head_count
    key_start = (lax.axis_index("seq") * tok_rows - halo_span * tok_rows).astype(jnp.int32)
    key_start = key_start.reshape(1)
    scale_power = jnp.left_shift(jnp.int32(1), scale_exponent[0]).astype(jnp.float32)
    grad_out = (cotangent.astype(jnp.float32) * scale_power).astype(jnp.bfloat16)

    master16 = qkv_master.astype(jnp.bfloat16).reshape(own_rows, kv_groups * group_cols)
    pair = 2 if kv_groups % 2 == 0 else 1
    pair_cols = pair * group_cols
    weights = lax.all_gather(master16, "seq", axis=0, tiled=True)
    blocks = row_blocks(normed, own_rows)
    forward = []
    for low in range(0, kv_groups, pair):
        qkv = dot_nn(normed, weights[:, low * group_cols : low * group_cols + pair_cols])
        kv, k_saved = [], []
        for g in range(pair):
            at = g * group_cols + q_cols
            k_raw = qkv[:, at : at + d]
            k_unit, k_factor = head_norm(k_raw)
            k_saved.append((k_raw, k_factor))
            kv += [k_unit.astype(jnp.bfloat16), qkv[:, at + d : at + 2 * d].astype(jnp.bfloat16)]
        kv = jnp.concatenate(kv, 1)
        kv_list = [shifted(kv, "seq", s) for s in range(halo_span, 0, -1)] + [kv]
        forward.append((qkv, kv_list, k_saved))
    outs, grads, sums, all_sent = [], [], [], []
    waiting = []

    def finish(gq, own, far_backs, k_raw, k_factor):
        for back in far_backs:
            back = after(back, outs[-1], *all_sent)
            own = own + back.astype(jnp.float32)
        gk = norm_back(k_raw, k_factor, own[:, :d])
        grad_qkv = jnp.concatenate(
            [gq, gk.astype(jnp.bfloat16), own[:, d:].astype(jnp.bfloat16)], 1
        )
        grad_qkv = lax.optimization_barrier(grad_qkv)
        grads.append(grad_qkv)
        earlier = sums[-2] if len(sums) >= 2 else ()
        sent, _, parts = reduce_rows(blocks, grad_qkv, earlier)
        all_sent.append(sent)
        sums.append(parts)

    for g in range(kv_groups):
        qkv, kv_list, k_saved = forward[g // pair]
        if len(waiting) == 3:
            finish(*waiting.pop(0))
        start = after(key_start, *(all_sent if all_sent else [x for f in forward for x in f[1]]))
        out, gq, own, *backs = group_attention(qkv, kv_list, grad_out, start, g % pair, g)
        outs.append(out)
        far_backs = [shifted(backs[s - 1], "seq", -s) for s in range(1, halo_span + 1)]
        waiting.append((gq, own, far_backs, *k_saved[g % pair]))
    while waiting:
        finish(*waiting.pop(0))
    grad_qkv = jnp.concatenate(grads, 1)

    def token_terms(rows_at, *earlier):
        rows = lax.dynamic_slice_in_dim(grad_qkv, rows_at, part_rows, 0)
        return dot_nt(after(rows, *earlier), weights)

    if head_count == 2:
        peer_terms = token_terms((1 - head_pos) * part_rows, *all_sent).astype(jnp.bfloat16)
        far_part = lax.ppermute(peer_terms, "head", [(0, 1), (1, 0)])
        d_tokens = lax.optimization_barrier(token_terms(head_pos * part_rows, peer_terms))
        d_tokens = d_tokens + far_part.astype(jnp.float32)
    else:
        d_tokens = lax.psum_scatter(
            dot_nt(grad_qkv, weights), "head", scatter_dimension=0, tiled=True
        )
    d_tokens = d_tokens.astype(jnp.bfloat16)
    attn_out = jnp.concatenate(outs, 1)
    own_flags = lax.dynamic_slice_in_dim(skip_flag, head_pos * kv_groups, kv_groups, 0)
    stepped = adam_step(
        own_flags, (1.0 / scale_power).reshape(1), sums, qkv_master, adam_first, adam_second
    )
    return (attn_out, d_tokens, *stepped)


def solution(mesh):
    return jax.shard_map(
        per_device,
        mesh=mesh,
        in_specs=(
            P("seq", None),
            P("seq", "head"),
            P("seq", "head", None),
            P("seq", "head", None),
            P("seq", "head", None),
            P(),
            P(),
        ),
        out_specs=(
            P("seq", "head"),
            P(("seq", "head"), None),
            P("seq", "head", None),
            P("seq", "head", None),
            P("seq", "head", None),
        ),
        check_vma=False,
    )
```
